1024 devices in a mesh: fsdp: 32 (over z, core), tp: 8 (over y), rep: 4 (over x).
Axes of the slice: x: 4, y: 8, z: 16, core: 2. Of those that a mesh axis runs over, the one named last changes fastest.
Arguments:
- momentum: bfloat16 [4, 8192, 16384], P('rep', 'fsdp', 'tp'), may hold values from -6 to 6
- gradient: bfloat16 [4, 8192, 16384], P('rep', 'fsdp', 'tp'), may hold values from -6 to 6
- basis: bfloat16 [16384, 256], P('tp'), may hold values from -6 to 6
Outputs:
- new_momentum: bfloat16 [4, 8192, 16384], P('rep', 'fsdp', 'tp')
- left_factor: bfloat16 [8192, 256], P('fsdp')
- next_basis: bfloat16 [16384, 256], P('tp')
The draws below stay inside these ranges and needn't reach their ends.
All inputs are finite; a program needn't handle non-finite values.
Results may differ from the reference program's by a relative error of at most 0.012.
Values sent between devices are 32-bit elements; how exact they have to be, the bound alone decides.
A program may use at most 32 MiB of HBM per device.

```python
import jax
import jax.numpy as jnp
from jax import lax

COLS = 16384
ROWS = 8192
RANK = 256
REPS = 4
N_REP = 4


def level_of(stream_key, shape, cuts, low, largest):
    level, own = 1.0, jax.random.fold_in(stream_key, 6)
    for dim, shards_of in cuts:
        steps = jnp.exp(jax.random.uniform(jax.random.fold_in(own, dim), (shards_of,), jnp.float32, low / len(cuts), largest / len(cuts)))
        level = level * jnp.repeat(steps, shape[dim] // shards_of).reshape([-1 if axis == dim else 1 for axis in range(len(shape))])
    return level


def bell_draw(key, dims, spread, limit, split=(), held_as=jnp.bfloat16):
    level = level_of(key, dims, split, -0.22, 0.18) if split else 1.0
    entries = jax.random.normal(key, dims, jnp.float32) * spread * level
    return jnp.minimum(jnp.maximum(entries, -limit), limit).astype(held_as)


def setup_inputs(seed: int = 0) -> dict:
    streams_of = jax.random.split(jax.random.key(seed), 4)
    return {
        "momentum": bell_draw(streams_of[0], (REPS, ROWS, COLS), 1.0, 6.0, ((0, 4), (1, 32), (2, 8))),
        "gradient": bell_draw(streams_of[1], (REPS, ROWS, COLS), 1.0, 6.0, ((0, 4), (1, 32), (2, 8))),
        "basis": bell_draw(streams_of[2], (COLS, RANK), 1.0, 6.0, ((0, 8),)),
    }


def mixed(momentum, gradient, index):
    return (momentum[index].astype(jnp.float32) + gradient[index].astype(jnp.float32)).astype(jnp.bfloat16)

def reference(momentum, gradient, basis):
    probe = jnp.zeros((ROWS, RANK), jnp.float32)
    for index in range(N_REP):
        probe = probe + jnp.dot(mixed(momentum, gradient, index).astype(jnp.float32), basis.astype(jnp.float32), preferred_element_type=jnp.float32)
    probe = probe / N_REP
    gram = jnp.dot(probe.T, probe, precision=lax.Precision.HIGHEST)
    lower = jnp.linalg.cholesky(gram)
    ortho = jax.scipy.linalg.solve_triangular(lower, probe.T, lower=True).T
    ortho_b = ortho.astype(jnp.bfloat16)
    left_factor = (ortho * ROWS ** 0.5).astype(jnp.bfloat16)
    back = jnp.zeros((COLS, RANK), jnp.float32)
    for index in range(N_REP):
        back = back + jnp.dot(mixed(momentum, gradient, index).T.astype(jnp.float32), ortho_b.astype(jnp.float32), preferred_element_type=jnp.float32)
    back = back / N_REP
    colsq = lax.optimization_barrier(jnp.sum(back * back, axis=0))
    next_basis = (back * (COLS ** 0.5 * lax.rsqrt(colsq + 1e-06))).astype(jnp.bfloat16)
    back_b = back.astype(jnp.bfloat16)
    updated = []
    for index in range(N_REP):
        feedback = jnp.dot(ortho_b.astype(jnp.float32), back_b.T.astype(jnp.float32), preferred_element_type=jnp.float32)
        mix = mixed(momentum, gradient, index).astype(jnp.float32)
        updated.append((mix - 0.2 * feedback).astype(jnp.bfloat16))
    return (jnp.stack(updated), left_factor, next_basis)
```

```python
import functools

import jax
import jax.numpy as jnp
from jax import lax
from jax.experimental import pallas as pl
from jax.experimental.pallas import tpu as pltpu
from jax.sharding import PartitionSpec as P

COLS = 16384
ROWS = 8192
RANK = 256
LANES = 128
PARTS = 4
HIGHEST = lax.Precision.HIGHEST
F32 = jnp.float32
BF16 = jnp.bfloat16


def rows_at(start, size):
    return pl.ds(pl.multiple_of(start, 8), size)


def dot_t(a, b, precision=None):
    return lax.dot_general(a, b, (((1,), (1,)), ((), ())), precision=precision, preferred_element_type=F32)


class Copies:
    def __init__(self, send_sem, recv_sem):
        self.send_sem, self.recv_sem, self.makers = send_sem, recv_sem, []

    def start(self, src, dst, device):
        slot = len(self.makers)

        def make():
            return pltpu.make_async_remote_copy(
                src_ref=src(), dst_ref=dst(), send_sem=self.send_sem.at[slot], recv_sem=self.recv_sem.at[slot],
                device_id=device, device_id_type=pl.DeviceIdType.MESH,
            )

        self.makers.append(make)
        make().start()
        return lambda: make().wait_recv()

    def finish(self):
        for make in self.makers:
            make().wait_send()


def ring_reduce_scatter(copies, ref, base, size, me, device, first, second):
    half = size // 2
    own = [base + lax.rem(me + d, 4) * size for d in range(4)]
    ahead = copies.start(lambda: ref.at[rows_at(own[2], half)], lambda: first.at[0], device(1))
    behind = copies.start(lambda: ref.at[rows_at(own[2] + half, half)], lambda: first.at[1], device(3))
    yield
    ahead()
    ref[rows_at(own[1], half)] += first[0]
    ahead = copies.start(lambda: ref.at[rows_at(own[1], size)], lambda: second.at[0], device(1))
    behind()
    ref[rows_at(own[3] + half, half)] += first[1]
    behind = copies.start(lambda: ref.at[rows_at(own[3], size)], lambda: second.at[1], device(3))
    yield
    ahead()
    behind()
    ref[rows_at(own[0], size)] += second[0] + second[1]


def ring_all_gather(copies, ref, base, size, me, device):
    half = size // 2
    own = [base + lax.rem(me + d, 4) * size for d in range(4)]
    mine = lambda: ref.at[rows_at(own[0], size)]
    ahead = copies.start(mine, mine, device(1))
    behind = copies.start(mine, mine, device(3))
    yield
    ahead()
    front = lambda: ref.at[rows_at(own[3], half)]
    ahead = copies.start(front, front, device(1))
    behind()
    back = lambda: ref.at[rows_at(own[1] + half, half)]
    behind = copies.start(back, back, device(3))
    yield
    ahead()
    behind()


def group_reduce_scatter(copies, ref, base, size, count, me, device, slots):
    def piece(d):
        return lambda: ref.at[rows_at(base + lax.rem(me + d, count) * size, size)]

    waits = [copies.start(piece(d), lambda d=d: slots.at[d - 1], device(d)) for d in range(1, count)]
    yield
    mine = rows_at(base + me * size, size)
    total = ref[mine]
    for d, wait in enumerate(waits):
        wait()
        total += slots[d]
    ref[mine] = total


def group_all_gather(copies, ref, base, size, count, me, device):
    mine = lambda: ref.at[rows_at(base + me * size, size)]
    waits = [copies.start(mine, mine, device(d)) for d in range(1, count)]
    yield
    for wait in waits:
        wait()


def group_sum(copies, slots, count, me, device):
    mine = lambda: slots.at[me]
    waits = [copies.start(mine, mine, device(d)) for d in range(1, count)]
    yield
    for wait in waits:
        wait()
    total = slots[0]
    for index in range(1, count):
        total += slots[index]
    return total


def factor_panel(p, x_ref, column_ref):
    row0 = p * 32
    side = p // 4
    lane = lax.broadcasted_iota(jnp.int32, (1, LANES), 1)
    for q in range(4):
        lane0 = lax.rem(p, 4) * 32 + 8 * q
        block = x_ref[side, rows_at(row0 + 8 * q, 32 - 8 * q), :]
        columns = []
        for k in range(8):
            at = jnp.full(block.shape, lane0 + k, jnp.int32)
            column = jnp.take_along_axis(block, at, axis=1, mode="promise_in_bounds")
            column_ref[k, 8 * q : 32, :] = column
            columns.append(column)
        a = {(i, k): column_ref[k, 8 * q + i : 8 * q + i + 1, :] for k in range(8) for i in range(k, 8)}
        low, scale = {}, []
        for k in range(8):
            scale.append(lax.rsqrt(a[k, k]))
            for i in range(k + 1, 8):
                low[i, k] = a[i, k] * scale[k]
            for j in range(k + 1, 8):
                for i in range(j, 8):
                    a[i, j] = a[i, j] - low[i, k] * low[j, k]
        inside = (lane >= lane0) & (lane < lane0 + 8)
        solved = []
        for h in range(2):
            here = inside & (side == h)
            rows = []
            for k in range(8):
                row = x_ref[h, pl.ds(row0 + 8 * q + k, 1), :]
                row = jnp.where(here, jnp.where(lane == lane0 + k, 1.0, 0.0), row)
                for j in range(k):
                    row = row - low[k, j] * rows[j]
                rows.append(row * scale[k])
            x_ref[h, rows_at(row0 + 8 * q, 8), :] = jnp.concatenate(rows, axis=0)
            solved.append(rows)
        if q < 3:
            left = 24 - 8 * q
            factor = []
            for k in range(8):
                column = columns[k][8:]
                for j in range(k):
                    column = column - factor[j] * low[k, j]
                factor.append(column * scale[k])
            for h in range(2):
                here = inside & (side == h)
                below = rows_at(row0 + 8 * q + 8, left)
                rest = jnp.where(here, 0.0, x_ref[h, below, :])
                for k in range(8):
                    rest = rest - factor[k] * solved[h][k]
                x_ref[h, below, :] = rest

    @pl.when(p < 7)
    def _():
        panel = rows_at(row0, 32)
        done = jnp.concatenate([x_ref[0, panel, :], x_ref[1, panel, :]], axis=1)
        along = lax.broadcasted_iota(jnp.int32, (32, RANK), 1) - row0
        down = lax.broadcasted_iota(jnp.int32, (32, RANK), 0)
        done = jnp.where((along > down) & (along < 32), 0.0, done)
        update = lax.dot_general(
            done, done, (((0,), (0,)), ((), ())), precision=HIGHEST, preferred_element_type=F32
        )
        lane0 = lax.rem(p, 4) * 32
        inside = (lane >= lane0) & (lane < lane0 + 32)
        below = lax.broadcasted_iota(jnp.int32, (RANK, LANES), 0) >= row0 + 32
        for h in range(2):
            old = x_ref[h]
            new = jnp.where(inside & (side == h), 0.0, old) - update[:, h * LANES : (h + 1) * LANES]
            x_ref[h] = jnp.where(below, new, old)


def step_kernel(
    sizes, cols,
    momentum, gradient, basis, new_momentum, left_factor, next_basis,
    mix, mix_t, probe, probe_first, probe_second, probe_slots, whole_probe,
    gram_part, gram_pair, gram_low, gram_high, gram, work, column_ref,
    share, pair, ring_first, ring_second, low_slots, high_slots, whole, back, ortho, squares,
    send_sem, recv_sem,
):
    n_x, n_y, n_low, n_high, n_core = sizes
    part = cols // PARTS
    f, t, r = lax.axis_index("fsdp"), lax.axis_index("tp"), lax.axis_index("rep")
    core, z = lax.rem(f, n_core), lax.div(f, n_core)
    low, high = lax.rem(z, n_low), lax.div(z, n_low)
    other = n_core - 1 - core

    def on_x(d):
        return {"rep": lax.rem(r + d, n_x)}

    def on_y(d):
        return {"tp": lax.rem(t + d, n_y)}

    def on_low(d):
        return {"fsdp": (high * n_low + lax.rem(low + d, n_low)) * n_core + core}

    def on_high(d):
        return {"fsdp": (lax.rem(high + d, n_high) * n_low + low) * n_core + core}

    sibling = {"fsdp": z * n_core + other}

    partners = [on_x(1), on_x(3)] if n_x > 1 else []
    partners += [on_y(d) for d in range(1, n_y)]
    partners += [on_low(d) for d in range(1, n_low)] + [on_high(d) for d in range(1, n_high)]
    partners += [sibling] if n_core > 1 else []
    barrier = pltpu.get_barrier_semaphore()
    for partner in partners:
        pl.semaphore_signal(barrier, inc=1, device_id=partner, device_id_type=pl.DeviceIdType.MESH)

    copies = Copies(send_sem, recv_sem)

    probe[...] = jnp.zeros_like(probe)

    @pl.loop(0, cols // 256)
    def _(j):
        here = pl.ds(pl.multiple_of(j * 256, 256), 256)
        block = (momentum[:, here].astype(F32) + gradient[:, here].astype(F32)).astype(BF16)
        mix[:, here] = block
        probe[...] += jnp.dot(block, basis[here, :], preferred_element_type=F32)

    pl.semaphore_wait(barrier, len(partners))

    def probe_sum():
        if n_x > 1:
            yield from ring_reduce_scatter(copies, probe, 0, 64, r, on_x, probe_first, probe_second)
        yield from group_reduce_scatter(copies, probe, r * 64, 64 // n_y, n_y, t, on_y, probe_slots)
        mine = rows_at(r * 64 + t * (64 // n_y), 64 // n_y)
        whole_probe[mine, :] = probe[mine, :] / 4
        yield from group_all_gather(copies, whole_probe, r * 64, 64 // n_y, n_y, t, on_y)
        if n_x > 1:
            yield from ring_all_gather(copies, whole_probe, 0, 64, r, on_x)

    steps = probe_sum()
    next(steps)

    @pl.loop(0, cols // 256)
    def _(j):
        here = pl.ds(pl.multiple_of(j * 256, 256), 256)
        mix_t[here, :] = mix[:, here].T

    for _ in steps:
        pass

    p32 = whole_probe[...]
    product = lax.dot_general(p32, p32, (((0,), (0,)), ((), ())), precision=HIGHEST, preferred_element_type=F32)
    gram_part[0] = product[:, :LANES]
    gram_part[1] = product[:, LANES:]

    def gram_sum():
        mine = rows_at(r * 64 + t * (64 // n_y), 64 // n_y)
        value = gram_part[core, mine, :]
        if n_core > 1:
            wait = copies.start(lambda: gram_part.at[other, mine], lambda: gram_pair, sibling)
            yield
            wait()
            value = value + gram_pair[...]
        gram_low[low] = value
        value = yield from group_sum(copies, gram_low, n_low, low, on_low)
        gram_high[high] = value
        value = yield from group_sum(copies, gram_high, n_high, high, on_high)
        gram[core, mine, :] = value
        own = gram.at[core]
        yield from group_all_gather(copies, own, r * 64, 64 // n_y, n_y, t, on_y)
        if n_x > 1:
            yield from ring_all_gather(copies, own, 0, 64, r, on_x)
        if n_core > 1:
            wait = copies.start(lambda: gram.at[core], lambda: gram.at[core], sibling)
            yield
            wait()

    gram_steps = gram_sum()
    next(gram_steps)

    terms = []
    rest = p32
    for _ in range(3):
        terms.append(rest.astype(BF16))
        rest = rest - terms[-1].astype(F32)

    def right_part(k):
        base = k * part

        @pl.loop(0, part // 256)
        def _(j):
            here = rows_at(base + j * 256, 256)
            block = mix_t[here, :]
            total = jnp.dot(block, terms[2], preferred_element_type=F32)
            total += jnp.dot(block, terms[1], preferred_element_type=F32)
            total += jnp.dot(block, terms[0], preferred_element_type=F32)
            share[0, here, :] = total[:, :LANES]
            share[1, here, :] = total[:, LANES:]

        chunk = rows_at(base, part)
        if n_core > 1:
            wait = copies.start(lambda: share.at[other, chunk], lambda: pair.at[chunk], sibling)
            yield
            wait()
            share[core, chunk, :] += pair[chunk, :]
        own, size = share.at[core], part // 4
        yield from ring_reduce_scatter(copies, own, base, size, r, on_x, ring_first.at[k], ring_second.at[k])
        at = base + r * size
        size //= n_low
        yield from group_reduce_scatter(copies, own, at, size, n_low, low, on_low, low_slots.at[k])
        at = at + low * size
        size //= n_high
        yield from group_reduce_scatter(copies, own, at, size, n_high, high, on_high, high_slots.at[k])
        mine = rows_at(at + high * size, size)
        whole[core, mine, :] = share[core, mine, :] / 4
        own = whole.at[core]
        yield from group_all_gather(copies, own, at, size, n_high, high, on_high)
        size *= n_high
        at = base + r * (part // 4)
        yield from group_all_gather(copies, own, at, size, n_low, low, on_low)
        yield from ring_all_gather(copies, own, base, part // 4, r, on_x)
        if n_core > 1:
            wait = copies.start(lambda: whole.at[core, chunk], lambda: whole.at[core, chunk], sibling)
            yield
            wait()

    right_steps = [right_part(k) for k in range(PARTS)]

    def advance(tick):
        for k in range(PARTS):
            if tick >= k:
                next(right_steps[k], None)

    tick = 0
    advance(tick)
    for _ in gram_steps:
        tick += 1
        advance(tick)

    work[...] = gram[...]

    def eliminate(p, carry):
        factor_panel(p, work, column_ref)
        return carry

    lax.fori_loop(0, 8, eliminate, 0)
    for _ in range(16):
        tick += 1
        advance(tick)

    row = lax.broadcasted_iota(jnp.int32, (RANK, RANK), 0)
    column = lax.broadcasted_iota(jnp.int32, (RANK, RANK), 1)
    inverse = jnp.where(column <= row, jnp.concatenate([work[0], work[1]], axis=1), 0.0)
    work[0] = inverse[:, :LANES]
    work[1] = inverse[:, LANES:]

    exact = dot_t(whole_probe[...], inverse, HIGHEST)
    left_factor[...] = (exact * ROWS**0.5).astype(BF16)
    ortho[...] = exact.astype(BF16)

    squares[t] = jnp.zeros((8, RANK), F32)

    @pl.loop(0, cols // 256)
    def _(j):
        here = rows_at(j * 256, 256)
        block = jnp.concatenate([whole[0, here, :], whole[1, here, :]], axis=1)
        lower = jnp.concatenate([work[0], work[1]], axis=1)
        value = dot_t(block, lower, HIGHEST)
        back[here, :] = value
        squares[t] += jnp.sum((value * value).reshape(32, 8, RANK), axis=0)

    sums = group_sum(copies, squares, n_y, t, on_y)
    next(sums)

    @pl.loop(0, cols // 256)
    def _(j):
        here = rows_at(j * 256, 256)
        at = pl.ds(pl.multiple_of(j * 256, 256), 256)
        feedback = dot_t(ortho[...], back[here, :].astype(BF16))
        new_momentum[:, at] = (mix[:, at].astype(F32) - 0.2 * feedback).astype(BF16)

    try:
        next(sums)
    except StopIteration as stop:
        total = stop.value
    colsq = jnp.sum(total, axis=0, keepdims=True)
    scale = COLS**0.5 * lax.rsqrt(colsq + 1e-06)

    @pl.loop(0, cols // 256)
    def _(j):
        here = rows_at(j * 256, 256)
        next_basis[here, :] = (back[here, :] * scale).astype(BF16)

    copies.finish()


def per_device(sizes, momentum, gradient, basis):
    n_x, n_y, n_low, n_high, n_core = sizes
    rows, cols = momentum.shape[1:]
    part = cols // PARTS
    quarter = part // 4
    low_size = quarter // n_low
    high_size = low_size // n_high
    probe_size = 64 // n_y
    n_copies = 512
    vmem = pltpu.VMEM
    scratch = [
        vmem((rows, cols), BF16),
        vmem((cols, rows), BF16),
        vmem((rows, RANK), F32),
        vmem((2, 32, RANK), F32),
        vmem((2, 64, RANK), F32),
        vmem((max(n_y - 1, 1), probe_size, RANK), F32),
        vmem((rows, RANK), F32),
        vmem((2, RANK, LANES), F32),
        vmem((probe_size, LANES), F32),
        vmem((n_low, probe_size, LANES), F32),
        vmem((n_high, probe_size, LANES), F32),
        vmem((2, RANK, LANES), F32),
        vmem((2, RANK, LANES), F32),
        vmem((8, 32, LANES), F32),
        vmem((2, cols, LANES), F32),
        vmem((cols, LANES), F32),
        vmem((PARTS, 2, quarter // 2, LANES), F32),
        vmem((PARTS, 2, quarter, LANES), F32),
        vmem((PARTS, max(n_low - 1, 1), low_size, LANES), F32),
        vmem((PARTS, max(n_high - 1, 1), high_size, LANES), F32),
        vmem((2, cols, LANES), F32),
        vmem((cols, RANK), F32),
        vmem((rows, RANK), BF16),
        vmem((n_y, 8, RANK), F32),
        pltpu.SemaphoreType.DMA((n_copies,)),
        pltpu.SemaphoreType.DMA((n_copies,)),
    ]
    out = pl.pallas_call(
        functools.partial(step_kernel, sizes, cols),
        out_shape=[
            jax.ShapeDtypeStruct((rows, cols), BF16),
            jax.ShapeDtypeStruct((rows, RANK), BF16),
            jax.ShapeDtypeStruct((cols, RANK), BF16),
        ],
        in_specs=[pl.BlockSpec(memory_space=pltpu.VMEM)] * 3,
        out_specs=[pl.BlockSpec(memory_space=pltpu.VMEM)] * 3,
        scratch_shapes=scratch,
        compiler_params=pltpu.CompilerParams(
            collective_id=0, has_side_effects=True, vmem_limit_bytes=48 * 2**20
        ),
        cost_estimate=pl.CostEstimate(flops=2**30, bytes_accessed=5 * 2**20, transcendentals=0),
    )(momentum[0], gradient[0], basis)
    return (out[0][None], out[1], out[2])


def solution(mesh):
    sizes = (4, 8, 4, 4, 2)
    in_specs = (P("rep", "fsdp", "tp"), P("rep", "fsdp", "tp"), P("tp", None))
    out_specs = (P("rep", "fsdp", "tp"), P("fsdp", None), P("tp", None))
    return jax.shard_map(
        functools.partial(per_device, sizes), mesh=mesh, in_specs=in_specs, out_specs=out_specs, check_vma=False
    )
```

```python
import functools

import jax
import jax.numpy as jnp
from jax import lax
from jax.experimental import pallas as pl
from jax.experimental.pallas import tpu as pltpu
from jax.sharding import PartitionSpec as P

COLS = 16384
ROWS = 8192
RANK = 256
LANES = 128
PARTS = 2
LOADS = 4
HIGHEST = lax.Precision.HIGHEST
F32 = jnp.float32
BF16 = jnp.bfloat16


def rows_at(start, size):
    return pl.ds(pl.multiple_of(start, 8), size)


def dot_t(a, b, precision=None):
    return lax.dot_general(a, b, (((1,), (1,)), ((), ())), precision=precision, preferred_element_type=F32)


class Copies:
    def __init__(self, send_sem, recv_sem):
        self.send_sem, self.recv_sem, self.makers, self.sent = send_sem, recv_sem, [], 0

    def start(self, src, dst, device):
        slot = len(self.makers)

        def make():
            return pltpu.make_async_remote_copy(
                src_ref=src(), dst_ref=dst(), send_sem=self.send_sem.at[slot], recv_sem=self.recv_sem.at[slot],
                device_id=device, device_id_type=pl.DeviceIdType.MESH,
            )

        self.makers.append(make)
        make().start()
        return lambda: make().wait_recv()

    def finish(self, keep=0):
        until = max(self.sent, len(self.makers) - keep)
        for make in self.makers[self.sent : until]:
            make().wait_send()
        self.sent = until


def ring_reduce_scatter(copies, ref, base, size, me, device, first, second):
    half = size // 2
    own = [base + lax.rem(me + d, 4) * size for d in range(4)]
    ahead = copies.start(lambda: ref.at[rows_at(own[2], half)], lambda: first.at[0], device(1))
    behind = copies.start(lambda: ref.at[rows_at(own[2] + half, half)], lambda: first.at[1], device(3))
    yield
    ahead()
    ref[rows_at(own[1], half)] += first[0]
    ahead = copies.start(lambda: ref.at[rows_at(own[1], size)], lambda: second.at[0], device(1))
    behind()
    ref[rows_at(own[3] + half, half)] += first[1]
    behind = copies.start(lambda: ref.at[rows_at(own[3], size)], lambda: second.at[1], device(3))
    yield
    ahead()
    behind()
    ref[rows_at(own[0], size)] += second[0] + second[1]


def ring_all_gather(copies, ref, base, size, me, device):
    half = size // 2
    own = [base + lax.rem(me + d, 4) * size for d in range(4)]
    mine = lambda: ref.at[rows_at(own[0], size)]
    ahead = copies.start(mine, mine, device(1))
    behind = copies.start(mine, mine, device(3))
    yield
    ahead()
    front = lambda: ref.at[rows_at(own[3], half)]
    ahead = copies.start(front, front, device(1))
    behind()
    back = lambda: ref.at[rows_at(own[1] + half, half)]
    behind = copies.start(back, back, device(3))
    yield
    ahead()
    behind()


def direct_reduce_scatter(copies, ref, piece, devices, slots, offset):
    waits = []
    for d, device in enumerate(devices):
        waits.append(copies.start(lambda d=d: ref.at[piece(d)], lambda d=d: slots.at[d], device))
    yield
    total = ref[offset]
    for d, wait in enumerate(waits):
        wait()
        total += slots[d]
    return total


def direct_all_gather(copies, ref, mine, devices):
    own = lambda: ref.at[mine]
    waits = [copies.start(own, own, device) for device in devices]
    yield
    for wait in waits:
        wait()


def direct_sum(copies, slots, count, me, devices):
    own = lambda: slots.at[me]
    waits = [copies.start(own, own, device) for device in devices]
    yield
    for wait in waits:
        wait()
    total = slots[0]
    for index in range(1, count):
        total += slots[index]
    return total


def factor_panel(p, x_ref, column_ref):
    row0 = p * 32
    side = p // 4
    lane = lax.broadcasted_iota(jnp.int32, (1, LANES), 1)
    for q in range(4):
        lane0 = lax.rem(p, 4) * 32 + 8 * q
        block = x_ref[side, rows_at(row0 + 8 * q, 32 - 8 * q), :]
        columns = []
        for k in range(8):
            at = jnp.full(block.shape, lane0 + k, jnp.int32)
            column = jnp.take_along_axis(block, at, axis=1, mode="promise_in_bounds")
            column_ref[k, 8 * q : 32, :] = column
            columns.append(column)
        a = {(i, k): column_ref[k, 8 * q + i : 8 * q + i + 1, :] for k in range(8) for i in range(k, 8)}
        low, scale = {}, []
        for k in range(8):
            scale.append(lax.rsqrt(a[k, k]))
            for i in range(k + 1, 8):
                low[i, k] = a[i, k] * scale[k]
            for j in range(k + 1, 8):
                for i in range(j, 8):
                    a[i, j] = a[i, j] - low[i, k] * low[j, k]
        inside = (lane >= lane0) & (lane < lane0 + 8)
        solved = []
        for h in range(2):
            here = inside & (side == h)
            rows = []
            for k in range(8):
                row = x_ref[h, pl.ds(row0 + 8 * q + k, 1), :]
                row = jnp.where(here, jnp.where(lane == lane0 + k, 1.0, 0.0), row)
                for j in range(k):
                    row = row - low[k, j] * rows[j]
                rows.append(row * scale[k])
            x_ref[h, rows_at(row0 + 8 * q, 8), :] = jnp.concatenate(rows, axis=0)
            solved.append(rows)
        if q < 3:
            left = 24 - 8 * q
            factor = []
            for k in range(8):
                column = columns[k][8:]
                for j in range(k):
                    column = column - factor[j] * low[k, j]
                factor.append(column * scale[k])
            for h in range(2):
                here = inside & (side == h)
                below = rows_at(row0 + 8 * q + 8, left)
                rest = jnp.where(here, 0.0, x_ref[h, below, :])
                for k in range(8):
                    rest = rest - factor[k] * solved[h][k]
                x_ref[h, below, :] = rest

    @pl.when(p < 7)
    def _():
        panel = rows_at(row0, 32)
        done = jnp.concatenate([x_ref[0, panel, :], x_ref[1, panel, :]], axis=1)
        along = lax.broadcasted_iota(jnp.int32, (32, RANK), 1) - row0
        down = lax.broadcasted_iota(jnp.int32, (32, RANK), 0)
        done = jnp.where((along > down) & (along < 32), 0.0, done)
        update = lax.dot_general(
            done, done, (((0,), (0,)), ((), ())), precision=HIGHEST, preferred_element_type=F32
        )
        lane0 = lax.rem(p, 4) * 32
        inside = (lane >= lane0) & (lane < lane0 + 32)
        below = lax.broadcasted_iota(jnp.int32, (RANK, LANES), 0) >= row0 + 32
        for h in range(2):
            old = x_ref[h]
            new = jnp.where(inside & (side == h), 0.0, old) - update[:, h * LANES : (h + 1) * LANES]
            x_ref[h] = jnp.where(below, new, old)


def step_kernel(
    sizes, cols,
    momentum_in, gradient_in, basis_in, new_momentum, left_factor, next_basis,
    momentum, gradient, basis, mix, mix_t, probe, probe_slots, whole_probe,
    gram_part, gram_pair, gram_slots, gram, work, column_ref,
    share, pair, ring_first, ring_second, z_slots, whole, back, ortho, square_pair, square_slots,
    load_sem, send_sem, recv_sem,
):
    n_x, n_y, n_z, n_core = sizes
    part = cols // PARTS
    f, t, r = lax.axis_index("fsdp"), lax.axis_index("tp"), lax.axis_index("rep")
    core, z = lax.rem(f, n_core), lax.div(f, n_core)
    other = n_core - 1 - core

    def on_x(d):
        return {"rep": lax.rem(r + d, n_x)}

    near = sorted(
        ((dx, dy) for dx in range(n_x) for dy in range(n_y) if dx or dy),
        key=lambda d: -min(d[0], n_x - d[0]) - min(d[1], n_y - d[1]),
    )
    plane = [{"rep": lax.rem(r + dx, n_x), "tp": lax.rem(t + dy, n_y)} for dx, dy in near]
    plane_rank = [lax.rem(r + dx, n_x) * n_y + lax.rem(t + dy, n_y) for dx, dy in near]
    far = sorted(range(1, n_z), key=lambda d: -min(d, n_z - d))
    line = [{"fsdp": lax.rem(z + d, n_z) * n_core + core} for d in far]
    line_rank = [lax.rem(z + d, n_z) for d in far]
    sibling = {"fsdp": z * n_core + other}
    rank = r * n_y + t

    partners = plane + line + [sibling]
    barrier = pltpu.get_barrier_semaphore()
    for partner in partners:
        pl.semaphore_signal(barrier, inc=1, device_id=partner, device_id_type=pl.DeviceIdType.MESH)

    block = cols // LOADS
    loads = []
    for j in range(LOADS):
        here = pl.ds(j * block, block)
        three = [
            pltpu.make_async_copy(momentum_in.at[:, here], momentum.at[:, here], load_sem.at[j, 0]),
            pltpu.make_async_copy(gradient_in.at[:, here], gradient.at[:, here], load_sem.at[j, 1]),
            pltpu.make_async_copy(basis_in.at[here, :], basis.at[here, :], load_sem.at[j, 2]),
        ]
        for load in three:
            load.start()
        loads.append(three)
    copies = Copies(send_sem, recv_sem)
    for j, three in enumerate(loads):
        for load in three:
            load.wait()
        here = pl.ds(j * block, block)
        value = (momentum[:, here].astype(F32) + gradient[:, here].astype(F32)).astype(BF16)
        mix[:, here] = value
        term = jnp.dot(value, basis[here, :], preferred_element_type=F32)
        probe[...] = term if j == 0 else probe[...] + term

    pl.semaphore_wait(barrier, len(partners))

    size = RANK // (n_x * n_y)
    mine = rows_at(rank * size, size)

    def probe_sum():
        total = yield from direct_reduce_scatter(
            copies, probe, lambda d: rows_at(plane_rank[d] * size, size), plane, probe_slots, mine
        )
        whole_probe[mine, :] = total / 4
        yield from direct_all_gather(copies, whole_probe, mine, plane)

    steps = probe_sum()
    next(steps)

    @pl.loop(0, cols // 256)
    def _(j):
        here = pl.ds(pl.multiple_of(j * 256, 256), 256)
        mix_t[here, :] = mix[:, here].T

    for _ in steps:
        copies.finish(len(plane))
    p32 = whole_probe[...]

    def gram_sum():
        product = lax.dot_general(
            p32, p32, (((0,), (0,)), ((), ())), precision=HIGHEST, preferred_element_type=F32
        )
        gram_part[0] = product[:, :LANES]
        gram_part[1] = product[:, LANES:]
        wait = copies.start(lambda: gram_part.at[other, mine], lambda: gram_pair, sibling)
        yield
        wait()
        gram_slots[z] = gram_part[core, mine, :] + gram_pair[...]
        gram[core, mine, :] = yield from direct_sum(copies, gram_slots, n_z, z, line)
        yield from direct_all_gather(copies, gram.at[core], mine, plane)
        wait = copies.start(lambda: gram.at[core], lambda: gram.at[core], sibling)
        yield
        wait()

    terms = []
    rest = p32
    for _ in range(3):
        terms.append(rest.astype(BF16))
        rest = rest - terms[-1].astype(F32)

    each = part // n_core
    quarter = each // 4
    piece = quarter // n_z

    def own_rows(k):
        return k * part + core * each + r * quarter

    def right_part(k):
        base = k * part

        @pl.loop(0, part // 256)
        def _(j):
            here = rows_at(base + j * 256, 256)
            value = mix_t[here, :]
            total = jnp.dot(value, terms[2], preferred_element_type=F32)
            total += jnp.dot(value, terms[1], preferred_element_type=F32)
            total += jnp.dot(value, terms[0], preferred_element_type=F32)
            share[here, :] = total

        half = base + core * each
        wait = copies.start(lambda: share.at[rows_at(base + other * each, each)], lambda: pair.at[k], sibling)
        yield
        wait()
        share[rows_at(half, each), :] += pair[k]
        yield from ring_reduce_scatter(copies, share, half, quarter, r, on_x, ring_first.at[k], ring_second.at[k])
        start = own_rows(k)
        here = rows_at(start + z * piece, piece)
        total = yield from direct_reduce_scatter(
            copies, share, lambda d: rows_at(start + line_rank[d] * piece, piece), line, z_slots.at[k], here
        )
        whole[here, :] = total / 4
        yield from direct_all_gather(copies, whole, here, line)

        def hand_on(offset, count):
            rows = lambda: whole.at[rows_at(offset, count)]
            return copies.start(rows, rows, sibling)

        def pass_on(offset, count, d):
            rows = lambda: whole.at[rows_at(offset, count)]
            return copies.start(rows, rows, on_x(d))

        at = [half + lax.rem(r + d, 4) * quarter for d in range(4)]
        ahead = pass_on(at[0], quarter, 1)
        behind = pass_on(at[0], quarter, 3)
        paired = [hand_on(at[0], quarter)]
        yield
        ahead()
        ahead = pass_on(at[3], quarter // 2, 1)
        behind()
        behind = pass_on(at[1] + quarter // 2, quarter // 2, 3)
        paired.append(hand_on(at[3], quarter))
        paired.append(hand_on(at[1], quarter))
        yield
        ahead()
        paired.append(hand_on(at[2], quarter // 2))
        behind()
        paired.append(hand_on(at[2] + quarter // 2, quarter // 2))
        yield
        for wait in paired:
            wait()

    gram_steps, right_steps = gram_sum(), [right_part(k) for k in range(PARTS)]

    def advance(order):
        for name in order:
            next(gram_steps if name == "g" else right_steps[int(name)], None)

    advance("01g0g1010g1")
    copies.finish(2)
    advance("0gg")

    work[...] = gram[...]

    def eliminate(p, carry):
        factor_panel(p, work, column_ref)
        return carry

    lax.fori_loop(0, 4, eliminate, 0)
    advance("1")
    lax.fori_loop(4, 8, eliminate, 0)

    row = lax.broadcasted_iota(jnp.int32, (RANK, RANK), 0)
    column = lax.broadcasted_iota(jnp.int32, (RANK, RANK), 1)
    inverse = jnp.where(column <= row, jnp.concatenate([work[0], work[1]], axis=1), 0.0)
    work[0] = inverse[:, :LANES]
    work[1] = inverse[:, LANES:]

    exact = dot_t(whole_probe[...], inverse, HIGHEST)
    left_factor[...] = (exact * ROWS**0.5).astype(BF16)
    ortho[...] = exact.astype(BF16)

    def back_of(start, count):
        lower = jnp.concatenate([work[0], work[1]], axis=1)
        return dot_t(whole[rows_at(start, count), :], lower, HIGHEST)

    advance("0")
    copies.finish(3)
    advance("1")

    squares = jnp.zeros((8, RANK), F32)
    for k in range(PARTS):
        value = back_of(own_rows(k), quarter)
        squares += jnp.sum((value * value).reshape(quarter // 8, 8, RANK), axis=0)
    squares = jnp.sum(squares, axis=0, keepdims=True)
    top = lax.broadcasted_iota(jnp.int32, (8, LANES), 0) == 0
    square_pair[0] = jnp.where(top, squares[:, :LANES], squares[:, LANES:])

    def square_sum():
        wait = copies.start(lambda: square_pair.at[0], lambda: square_pair.at[1], sibling)
        yield
        wait()
        square_slots[rank] = square_pair[0] + square_pair[1]
        return (yield from direct_sum(copies, square_slots, n_x * n_y, rank, plane))

    square_steps = square_sum()
    next(square_steps)
    advance("0")
    next(square_steps)

    def finish_part(k):
        @pl.loop(k * part // 256, (k + 1) * part // 256)
        def _(j):
            here = rows_at(j * 256, 256)
            at = pl.ds(pl.multiple_of(j * 256, 256), 256)
            value = back_of(j * 256, 256)
            back[here, :] = value
            feedback = dot_t(ortho[...], value.astype(BF16))
            new_momentum[:, at] = (mix[:, at].astype(F32) - 0.2 * feedback).astype(BF16)

    advance("10")
    copies.finish(10)
    advance("0")
    finish_part(0)
    advance("1")
    copies.finish(2)
    advance("1")
    finish_part(1)

    try:
        next(square_steps)
    except StopIteration as stop:
        total = stop.value
    colsq = jnp.concatenate([total[:1], total[1:2]], axis=1)
    scale = COLS**0.5 * lax.rsqrt(colsq + 1e-06)

    @pl.loop(0, cols // 256)
    def _(j):
        here = rows_at(j * 256, 256)
        next_basis[here, :] = (back[here, :] * scale).astype(BF16)

    copies.finish()


def per_device(sizes, momentum, gradient, basis):
    n_x, n_y, n_z, n_core = sizes
    rows, cols = momentum.shape[1:]
    part = cols // PARTS
    each = part // n_core
    quarter = each // 4
    size = RANK // (n_x * n_y)
    n_copies = 256
    vmem = pltpu.VMEM
    scratch = [
        vmem((rows, cols), BF16),
        vmem((rows, cols), BF16),
        vmem((cols, RANK), BF16),
        vmem((rows, cols), BF16),
        vmem((cols, rows), BF16),
        vmem((rows, RANK), F32),
        vmem((n_x * n_y - 1, size, RANK), F32),
        vmem((rows, RANK), F32),
        vmem((2, RANK, LANES), F32),
        vmem((size, LANES), F32),
        vmem((n_z, size, LANES), F32),
        vmem((2, RANK, LANES), F32),
        vmem((2, RANK, LANES), F32),
        vmem((8, 32, LANES), F32),
        vmem((cols, RANK), F32),
        vmem((PARTS, each, RANK), F32),
        vmem((PARTS, 2, quarter // 2, RANK), F32),
        vmem((PARTS, 2, quarter, RANK), F32),
        vmem((PARTS, max(n_z - 1, 1), quarter // n_z, RANK), F32),
        vmem((cols, RANK), F32),
        vmem((cols, RANK), F32),
        vmem((rows, RANK), BF16),
        vmem((2, 8, LANES), F32),
        vmem((n_x * n_y, 8, LANES), F32),
        pltpu.SemaphoreType.DMA((LOADS, 3)),
        pltpu.SemaphoreType.DMA((n_copies,)),
        pltpu.SemaphoreType.DMA((n_copies,)),
    ]
    out = pl.pallas_call(
        functools.partial(step_kernel, sizes, cols),
        out_shape=[
            jax.ShapeDtypeStruct((rows, cols), BF16),
            jax.ShapeDtypeStruct((rows, RANK), BF16),
            jax.ShapeDtypeStruct((cols, RANK), BF16),
        ],
        in_specs=[pl.BlockSpec(memory_space=pl.ANY)] * 3,
        out_specs=[pl.BlockSpec(memory_space=pltpu.VMEM)] * 3,
        scratch_shapes=scratch,
        compiler_params=pltpu.CompilerParams(
            collective_id=0, has_side_effects=True, vmem_limit_bytes=48 * 2**20
        ),
        cost_estimate=pl.CostEstimate(flops=2**30, bytes_accessed=5 * 2**20, transcendentals=0),
    )(momentum[0], gradient[0], basis)
    return (out[0][None], out[1], out[2])


def solution(mesh):
    sizes = (4, 8, 16, 2)
    in_specs = (P("rep", "fsdp", "tp"), P("rep", "fsdp", "tp"), P("tp", None))
    out_specs = (P("rep", "fsdp", "tp"), P("fsdp", None), P("tp", None))
    return jax.shard_map(
        functools.partial(per_device, sizes), mesh=mesh, in_specs=in_specs, out_specs=out_specs, check_vma=False
    )
```

```python
import functools

import jax
import jax.numpy as jnp
from jax import lax
from jax.experimental import pallas as pl
from jax.experimental.pallas import tpu as pltpu
from jax.sharding import PartitionSpec as P

COLS = 16384
ROWS = 8192
RANK = 256
LANES = 128
PARTS = 2
LOADS = 4
HIGHEST = lax.Precision.HIGHEST
F32 = jnp.float32
BF16 = jnp.bfloat16


def rows_at(start, size):
    return pl.ds(pl.multiple_of(start, 8), size)


def dot_t(a, b, precision=None):
    return lax.dot_general(a, b, (((1,), (1,)), ((), ())), precision=precision, preferred_element_type=F32)


class Copies:
    def __init__(self, send_sem, recv_sem):
        self.send_sem, self.recv_sem, self.makers, self.sent = send_sem, recv_sem, [], 0

    def start(self, src, dst, device):
        slot = len(self.makers)

        def make():
            return pltpu.make_async_remote_copy(
                src_ref=src(), dst_ref=dst(), send_sem=self.send_sem.at[slot], recv_sem=self.recv_sem.at[slot],
                device_id=device, device_id_type=pl.DeviceIdType.MESH,
            )

        self.makers.append(make)
        make().start()
        return lambda: make().wait_recv()

    def finish(self, keep=0):
        until = max(self.sent, len(self.makers) - keep)
        for make in self.makers[self.sent : until]:
            make().wait_send()
        self.sent = until


def ring_reduce_scatter(copies, ref, base, size, me, device, first, second):
    half = size // 2
    own = [base + lax.rem(me + d, 4) * size for d in range(4)]
    ahead = copies.start(lambda: ref.at[rows_at(own[2], half)], lambda: first.at[0], device(1))
    behind = copies.start(lambda: ref.at[rows_at(own[2] + half, half)], lambda: first.at[1], device(3))
    yield
    ahead()
    ref[rows_at(own[1], half)] += first[0]
    ahead = copies.start(lambda: ref.at[rows_at(own[1], size)], lambda: second.at[0], device(1))
    behind()
    ref[rows_at(own[3] + half, half)] += first[1]
    behind = copies.start(lambda: ref.at[rows_at(own[3], size)], lambda: second.at[1], device(3))
    yield
    ahead()
    behind()
    ref[rows_at(own[0], size)] += second[0] + second[1]


def ring_all_gather(copies, ref, base, size, me, device):
    half = size // 2
    own = [base + lax.rem(me + d, 4) * size for d in range(4)]
    mine = lambda: ref.at[rows_at(own[0], size)]
    ahead = copies.start(mine, mine, device(1))
    behind = copies.start(mine, mine, device(3))
    yield
    ahead()
    front = lambda: ref.at[rows_at(own[3], half)]
    ahead = copies.start(front, front, device(1))
    behind()
    back = lambda: ref.at[rows_at(own[1] + half, half)]
    behind = copies.start(back, back, device(3))
    yield
    ahead()
    behind()


def direct_reduce_scatter(copies, ref, piece, devices, slots, offset):
    waits = []
    for d, device in enumerate(devices):
        waits.append(copies.start(lambda d=d: ref.at[piece(d)], lambda d=d: slots.at[d], device))
    yield
    total = ref[offset]
    for d, wait in enumerate(waits):
        wait()
        total += slots[d]
    return total


def direct_all_gather(copies, ref, mine, devices):
    own = lambda: ref.at[mine]
    waits = [copies.start(own, own, device) for device in devices]
    yield
    for wait in waits:
        wait()


def direct_sum(copies, slots, count, me, devices):
    own = lambda: slots.at[me]
    waits = [copies.start(own, own, device) for device in devices]
    yield
    for wait in waits:
        wait()
    total = slots[0]
    for index in range(1, count):
        total += slots[index]
    return total


def factor_panel(p, x_ref, column_ref):
    row0 = p * 32
    side = p // 4
    lane = lax.broadcasted_iota(jnp.int32, (1, LANES), 1)
    for q in range(4):
        lane0 = lax.rem(p, 4) * 32 + 8 * q
        block = x_ref[side, rows_at(row0 + 8 * q, 32 - 8 * q), :]
        columns = []
        for k in range(8):
            at = jnp.full(block.shape, lane0 + k, jnp.int32)
            column = jnp.take_along_axis(block, at, axis=1, mode="promise_in_bounds")
            column_ref[k, 8 * q : 32, :] = column
            columns.append(column)
        a = {(i, k): column_ref[k, 8 * q + i : 8 * q + i + 1, :] for k in range(8) for i in range(k, 8)}
        low, scale = {}, []
        for k in range(8):
            scale.append(lax.rsqrt(a[k, k]))
            for i in range(k + 1, 8):
                low[i, k] = a[i, k] * scale[k]
            for j in range(k + 1, 8):
                for i in range(j, 8):
                    a[i, j] = a[i, j] - low[i, k] * low[j, k]
        inside = (lane >= lane0) & (lane < lane0 + 8)
        solved = []
        for h in range(2):
            here = inside & (side == h)
            rows = []
            for k in range(8):
                row = x_ref[h, pl.ds(row0 + 8 * q + k, 1), :]
                row = jnp.where(here, jnp.where(lane == lane0 + k, 1.0, 0.0), row)
                for j in range(k):
                    row = row - low[k, j] * rows[j]
                rows.append(row * scale[k])
            x_ref[h, rows_at(row0 + 8 * q, 8), :] = jnp.concatenate(rows, axis=0)
            solved.append(rows)
        if q < 3:
            left = 24 - 8 * q
            factor = []
            for k in range(8):
                column = columns[k][8:]
                for j in range(k):
                    column = column - factor[j] * low[k, j]
                factor.append(column * scale[k])
            for h in range(2):
                here = inside & (side == h)
                below = rows_at(row0 + 8 * q + 8, left)
                rest = jnp.where(here, 0.0, x_ref[h, below, :])
                for k in range(8):
                    rest = rest - factor[k] * solved[h][k]
                x_ref[h, below, :] = rest

    @pl.when(p < 7)
    def _():
        panel = rows_at(row0, 32)
        done = jnp.concatenate([x_ref[0, panel, :], x_ref[1, panel, :]], axis=1)
        along = lax.broadcasted_iota(jnp.int32, (32, RANK), 1) - row0
        down = lax.broadcasted_iota(jnp.int32, (32, RANK), 0)
        done = jnp.where((along > down) & (along < 32), 0.0, done)
        update = lax.dot_general(
            done, done, (((0,), (0,)), ((), ())), precision=HIGHEST, preferred_element_type=F32
        )
        lane0 = lax.rem(p, 4) * 32
        inside = (lane >= lane0) & (lane < lane0 + 32)
        below = lax.broadcasted_iota(jnp.int32, (RANK, LANES), 0) >= row0 + 32
        for h in range(2):
            old = x_ref[h]
            new = jnp.where(inside & (side == h), 0.0, old) - update[:, h * LANES : (h + 1) * LANES]
            x_ref[h] = jnp.where(below, new, old)


def step_kernel(
    sizes, cols,
    momentum_in, gradient_in, basis_in, new_momentum, left_factor, next_basis,
    momentum, gradient, basis, mix, mix_t, probe, probe_slots, whole_probe,
    gram_part, gram_pair, gram_slots, gram, work, column_ref,
    share, pair, ring_first, ring_second, mean, mean_first, mean_second, z_slots, whole, back, ortho, square_pair, square_slots,
    load_sem, send_sem, recv_sem,
):
    n_x, n_y, n_z, n_core = sizes
    part = cols // PARTS
    f, t, r = lax.axis_index("fsdp"), lax.axis_index("tp"), lax.axis_index("rep")
    core, z = lax.rem(f, n_core), lax.div(f, n_core)
    other = n_core - 1 - core

    def on_x(d):
        return {"rep": lax.rem(r + d, n_x)}

    near = sorted(
        ((dx, dy) for dx in range(n_x) for dy in range(n_y) if dx or dy),
        key=lambda d: -min(d[0], n_x - d[0]) - min(d[1], n_y - d[1]),
    )
    plane = [{"rep": lax.rem(r + dx, n_x), "tp": lax.rem(t + dy, n_y)} for dx, dy in near]
    plane_rank = [lax.rem(r + dx, n_x) * n_y + lax.rem(t + dy, n_y) for dx, dy in near]
    far = sorted(range(1, n_z), key=lambda d: -min(d, n_z - d))
    line = [{"fsdp": lax.rem(z + d, n_z) * n_core + core} for d in far]
    line_rank = [lax.rem(z + d, n_z) for d in far]
    sibling = {"fsdp": z * n_core + other}
    rank = r * n_y + t

    partners = plane + line + [sibling]
    barrier = pltpu.get_barrier_semaphore()
    for partner in partners:
        pl.semaphore_signal(barrier, inc=1, device_id=partner, device_id_type=pl.DeviceIdType.MESH)

    block = cols // LOADS
    loads = []
    for j in range(LOADS):
        here = pl.ds(j * block, block)
        three = [
            pltpu.make_async_copy(momentum_in.at[:, here], momentum.at[:, here], load_sem.at[j, 0]),
            pltpu.make_async_copy(gradient_in.at[:, here], gradient.at[:, here], load_sem.at[j, 1]),
            pltpu.make_async_copy(basis_in.at[here, :], basis.at[here, :], load_sem.at[j, 2]),
        ]
        for load in three:
            load.start()
        loads.append(three)
    copies = Copies(send_sem, recv_sem)
    for j, three in enumerate(loads):
        for load in three:
            load.wait()
        here = pl.ds(j * block, block)
        value = (momentum[:, here].astype(F32) + gradient[:, here].astype(F32)).astype(BF16)
        mix[:, here] = value
        term = jnp.dot(value, basis[here, :], preferred_element_type=F32)
        probe[...] = term if j == 0 else probe[...] + term

    pl.semaphore_wait(barrier, len(partners))

    size = RANK // (n_x * n_y)
    mine = rows_at(rank * size, size)

    def probe_sum():
        total = yield from direct_reduce_scatter(
            copies, probe, lambda d: rows_at(plane_rank[d] * size, size), plane, probe_slots, mine
        )
        whole_probe[mine, :] = total / 4
        yield from direct_all_gather(copies, whole_probe, mine, plane)

    steps = probe_sum()
    next(steps)

    @pl.loop(0, cols // 256)
    def _(j):
        here = pl.ds(pl.multiple_of(j * 256, 256), 256)
        mix_t[here, :] = mix[:, here].T

    mean[...] = mix_t[:part, :].astype(F32)
    mean_steps = ring_reduce_scatter(copies, mean, 0, part // 4, r, on_x, mean_first, mean_second)
    next(mean_steps)
    next(steps)
    next(mean_steps)
    copies.finish(2)
    next(steps, None)
    p32 = whole_probe[...]
    next(mean_steps, None)

    def gram_sum():
        product = lax.dot_general(
            p32, p32, (((0,), (0,)), ((), ())), precision=HIGHEST, preferred_element_type=F32
        )
        gram_part[0] = product[:, :LANES]
        gram_part[1] = product[:, LANES:]
        wait = copies.start(lambda: gram_part.at[other, mine], lambda: gram_pair, sibling)
        yield
        wait()
        gram_slots[z] = gram_part[core, mine, :] + gram_pair[...]
        gram[core, mine, :] = yield from direct_sum(copies, gram_slots, n_z, z, line)
        yield from direct_all_gather(copies, gram.at[core], mine, plane)
        wait = copies.start(lambda: gram.at[core], lambda: gram.at[core], sibling)
        yield
        wait()

    terms = []
    rest = p32
    for _ in range(3):
        terms.append(rest.astype(BF16))
        rest = rest - terms[-1].astype(F32)

    each = part // n_core
    quarter = each // 4
    piece = quarter // n_z

    def rows_of(k, d):
        at = lax.rem(r + d, 4)
        if k == 0:
            return at * (quarter * n_core) + core * quarter
        return k * part + core * each + at * quarter

    def right_part(k):
        if k == 0:
            own = r * (quarter * n_core)
            share[rows_at(own, quarter * n_core), :] = jnp.dot(
                mean[rows_at(own, quarter * n_core), :], p32, precision=HIGHEST, preferred_element_type=F32
            )
            start = own + core * quarter
            wait = copies.start(
                lambda: share.at[rows_at(own + other * quarter, quarter)],
                lambda: pair.at[0, pl.ds(0, quarter)],
                sibling,
            )
            yield
            wait()
            share[rows_at(start, quarter), :] += pair[0, :quarter]
            yield from spread(k, start)
            return
        base = k * part
        half, away = base + core * each, base + other * each

        def terms_of(start):
            @pl.loop(0, each // 256)
            def _(j):
                here = rows_at(start + j * 256, 256)
                value = mix_t[here, :]
                total = jnp.dot(value, terms[2], preferred_element_type=F32)
                total += jnp.dot(value, terms[1], preferred_element_type=F32)
                total += jnp.dot(value, terms[0], preferred_element_type=F32)
                share[here, :] = total

        terms_of(away)
        wait = copies.start(lambda: share.at[rows_at(away, each)], lambda: pair.at[k], sibling)
        terms_of(half)
        yield
        wait()
        share[rows_at(half, each), :] += pair[k]
        yield from ring_reduce_scatter(copies, share, half, quarter, r, on_x, ring_first.at[k], ring_second.at[k])
        yield from spread(k, rows_of(k, 0))

    def spread(k, start):
        here = rows_at(start + z * piece, piece)
        total = yield from direct_reduce_scatter(
            copies, share, lambda d: rows_at(start + line_rank[d] * piece, piece), line, z_slots.at[k], here
        )
        whole[here, :] = total / 4
        yield from direct_all_gather(copies, whole, here, line)

        def hand_on(offset, count):
            rows = lambda: whole.at[rows_at(offset, count)]
            return copies.start(rows, rows, sibling)

        def pass_on(offset, count, d):
            rows = lambda: whole.at[rows_at(offset, count)]
            return copies.start(rows, rows, on_x(d))

        at = [rows_of(k, d) for d in range(4)]
        ahead = pass_on(at[0], quarter, 1)
        behind = pass_on(at[0], quarter, 3)
        paired = [hand_on(at[0], quarter)]
        yield
        ahead()
        ahead = pass_on(at[3], quarter // 2, 1)
        behind()
        behind = pass_on(at[1] + quarter // 2, quarter // 2, 3)
        paired.append(hand_on(at[3], quarter))
        paired.append(hand_on(at[1], quarter))
        yield
        ahead()
        paired.append(hand_on(at[2], quarter // 2))
        behind()
        paired.append(hand_on(at[2] + quarter // 2, quarter // 2))
        yield
        for wait in paired:
            wait()

    gram_steps, right_steps = gram_sum(), [right_part(k) for k in range(PARTS)]

    def advance(order):
        for name in order:
            next(gram_steps if name == "g" else right_steps[int(name)], None)

    advance("1g0g101g10")
    copies.finish(len(line))
    advance("gg")

    work[...] = gram[...]

    def eliminate(p, carry):
        factor_panel(p, work, column_ref)
        return carry

    lax.fori_loop(0, 4, eliminate, 0)
    advance("10")
    lax.fori_loop(4, 8, eliminate, 0)

    row = lax.broadcasted_iota(jnp.int32, (RANK, RANK), 0)
    column = lax.broadcasted_iota(jnp.int32, (RANK, RANK), 1)
    inverse = jnp.where(column <= row, jnp.concatenate([work[0], work[1]], axis=1), 0.0)
    work[0] = inverse[:, :LANES]
    work[1] = inverse[:, LANES:]

    exact = dot_t(whole_probe[...], inverse, HIGHEST)
    left_factor[...] = (exact * ROWS**0.5).astype(BF16)
    ortho[...] = exact.astype(BF16)

    def back_of(start, count):
        lower = jnp.concatenate([work[0], work[1]], axis=1)
        return dot_t(whole[rows_at(start, count), :], lower, HIGHEST)

    advance("0")
    copies.finish(4)
    advance("01")

    squares = jnp.zeros((8, RANK), F32)
    for k in range(PARTS):
        value = back_of(rows_of(k, 0), quarter)
        squares += jnp.sum((value * value).reshape(quarter // 8, 8, RANK), axis=0)
    squares = jnp.sum(squares, axis=0, keepdims=True)
    top = lax.broadcasted_iota(jnp.int32, (8, LANES), 0) == 0
    square_pair[0] = jnp.where(top, squares[:, :LANES], squares[:, LANES:])

    def square_sum():
        wait = copies.start(lambda: square_pair.at[0], lambda: square_pair.at[1], sibling)
        yield
        wait()
        square_slots[rank] = square_pair[0] + square_pair[1]
        return (yield from direct_sum(copies, square_slots, n_x * n_y, rank, plane))

    def finish_part(k):
        @pl.loop(k * part // 256, (k + 1) * part // 256)
        def _(j):
            here = rows_at(j * 256, 256)
            at = pl.ds(pl.multiple_of(j * 256, 256), 256)
            value = back_of(j * 256, 256)
            back[here, :] = value
            feedback = dot_t(ortho[...], value.astype(BF16))
            new_momentum[:, at] = (mix[:, at].astype(F32) - 0.2 * feedback).astype(BF16)

    square_steps = square_sum()
    next(square_steps)
    advance("0")
    next(square_steps)
    finish_part(0)
    advance("1")
    copies.finish(4)
    advance("11")
    finish_part(1)

    try:
        next(square_steps)
    except StopIteration as stop:
        total = stop.value
    colsq = jnp.concatenate([total[:1], total[1:2]], axis=1)
    scale = COLS**0.5 * lax.rsqrt(colsq + 1e-06)

    @pl.loop(0, cols // 256)
    def _(j):
        here = rows_at(j * 256, 256)
        next_basis[here, :] = (back[here, :] * scale).astype(BF16)

    copies.finish()


def per_device(sizes, momentum, gradient, basis):
    n_x, n_y, n_z, n_core = sizes
    rows, cols = momentum.shape[1:]
    part = cols // PARTS
    each = part // n_core
    quarter = each // 4
    size = RANK // (n_x * n_y)
    n_copies = 256
    vmem = pltpu.VMEM
    scratch = [
        vmem((rows, cols), BF16),
        vmem((rows, cols), BF16),
        vmem((cols, RANK), BF16),
        vmem((rows, cols), BF16),
        vmem((cols, rows), BF16),
        vmem((rows, RANK), F32),
        vmem((n_x * n_y - 1, size, RANK), F32),
        vmem((rows, RANK), F32),
        vmem((2, RANK, LANES), F32),
        vmem((size, LANES), F32),
        vmem((n_z, size, LANES), F32),
        vmem((2, RANK, LANES), F32),
        vmem((2, RANK, LANES), F32),
        vmem((8, 32, LANES), F32),
        vmem((cols, RANK), F32),
        vmem((PARTS, each, RANK), F32),
        vmem((PARTS, 2, quarter // 2, RANK), F32),
        vmem((PARTS, 2, quarter, RANK), F32),
        vmem((part, RANK), F32),
        vmem((2, part // 8, RANK), F32),
        vmem((2, part // 4, RANK), F32),
        vmem((PARTS, max(n_z - 1, 1), quarter // n_z, RANK), F32),
        vmem((cols, RANK), F32),
        vmem((cols, RANK), F32),
        vmem((rows, RANK), BF16),
        vmem((2, 8, LANES), F32),
        vmem((n_x * n_y, 8, LANES), F32),
        pltpu.SemaphoreType.DMA((LOADS, 3)),
        pltpu.SemaphoreType.DMA((n_copies,)),
        pltpu.SemaphoreType.DMA((n_copies,)),
    ]
    out = pl.pallas_call(
        functools.partial(step_kernel, sizes, cols),
        out_shape=[
            jax.ShapeDtypeStruct((rows, cols), BF16),
            jax.ShapeDtypeStruct((rows, RANK), BF16),
            jax.ShapeDtypeStruct((cols, RANK), BF16),
        ],
        in_specs=[pl.BlockSpec(memory_space=pl.ANY)] * 3,
        out_specs=[pl.BlockSpec(memory_space=pltpu.VMEM)] * 3,
        scratch_shapes=scratch,
        compiler_params=pltpu.CompilerParams(
            collective_id=0, has_side_effects=True, vmem_limit_bytes=48 * 2**20
        ),
        cost_estimate=pl.CostEstimate(flops=2**30, bytes_accessed=5 * 2**20, transcendentals=0),
    )(momentum[0], gradient[0], basis)
    return (out[0][None], out[1], out[2])


def solution(mesh):
    sizes = (4, 8, 16, 2)
    in_specs = (P("rep", "fsdp", "tp"), P("rep", "fsdp", "tp"), P("tp", None))
    out_specs = (P("rep", "fsdp", "tp"), P("fsdp", None), P("tp", None))
    return jax.shard_map(
        functools.partial(per_device, sizes), mesh=mesh, in_specs=in_specs, out_specs=out_specs, check_vma=False
    )
```
